256 devices in a mesh: orb: 32 (over y, x, core), aux: 8 (over z).
Axes of the slice: x: 4, y: 4, z: 8, core: 2. Of those that a mesh axis runs over, the one named last changes fastest.
Arguments:
- coulomb_blocks: bfloat16 [256, 768, 768], P(None, 'orb'), may hold values from -0.21875 to 0.21875
- occupancy: int32 [96, 96], P('orb'), may hold values 0 or 1
- green_occ: bfloat16 [768, 768], replicated, may hold values from -0.21875 to 0.21875
- green_virt: bfloat16 [768, 768], P(None, 'aux'), may hold values from -0.21875 to 0.21875
Outputs:
- polarizability: float32 [256, 256], P('aux', 'orb')
The draws below stay inside these ranges and needn't reach their ends.
All inputs are finite; a program needn't handle non-finite values. No bound on the sum of `occupancy` on one device may be relied on, other than what follows from the above.
Results may differ from the reference program's by a relative error of at most 0.0041.
Values may be sent and summed in bfloat16 or wider, within the bound.
No kernel may reach another device: no remote copies, remote signals or barrier semaphores. Data moves between devices by JAX's collectives and lax.ppermute only.
A program may use at most 128 MiB of HBM per device.

```python
import jax
import jax.numpy as jnp

BLK = 8
NAO = 768
NAUX = 256


def touch_ends(drawn, stream_key, low, top_value):
    longest = drawn.shape.index(max(drawn.shape))
    spots = []
    for shift in (0, 1):
        where = [jax.random.randint(jax.random.fold_in(stream_key, axis), (), 0, length) for axis, length in enumerate(drawn.shape)]
        where[longest] = (where[longest] + shift) % drawn.shape[longest]
        spots.append(tuple(where))
    return drawn.at[spots[0]].set(low).at[spots[1]].set(top_value)


def block_scale(stream_key, dims, cuts, smallest, high):
    factor_of = 1.0
    for axis_at, parts in cuts:
        steps = jax.random.uniform(jax.random.fold_in(jax.random.fold_in(stream_key, 6), axis_at), (parts,), jnp.float32, smallest / len(cuts), high / len(cuts))
        factor_of = factor_of * jnp.repeat(jnp.exp(steps), dims[axis_at] // parts).reshape((-1,) + (1,) * (len(dims) - 1 - axis_at))
    return factor_of


def normal_values(own_key, shape, spread, bound, cuts=(), kind=jnp.bfloat16):
    result = jax.random.normal(own_key, shape, jnp.float32) * spread
    if len(cuts) > 0:
        result = block_scale(own_key, shape, cuts, -0.22, 0.18) * result
    return jnp.clip(result, min=-bound, max=bound).astype(kind)


def setup_inputs(seed: int = 0) -> dict:
    key_list = jax.random.split(jax.random.key(seed), 5)
    return {
        "coulomb_blocks": normal_values(key_list[0], (NAUX, NAO, NAO), NAO ** -0.5, 0.21875, ((1, 32),)),
        "occupancy": touch_ends((jax.random.randint(key_list[1], (NAO // BLK, NAO // BLK), 0, 4) < 3).astype(jnp.int32), jax.random.fold_in(key_list[1], 1), 0, 1),
        "green_occ": normal_values(key_list[2], (NAO, NAO), NAO ** -0.5, 0.21875),
        "green_virt": normal_values(key_list[3], (NAO, NAO), NAO ** -0.5, 0.21875, ((1, 8),)),
    }


def reference(coulomb_blocks, occupancy, green_occ, green_virt):
    naux = coulomb_blocks.shape[0]
    nao = coulomb_blocks.shape[1]
    mask = jnp.repeat(jnp.repeat(occupancy, BLK, 0), BLK, 1).astype(jnp.bfloat16)
    screened = coulomb_blocks * mask[None, :, :]
    half_virt = jnp.dot(screened.reshape(naux * nao, nao), green_virt, preferred_element_type=jnp.float32)
    half_virt = half_virt.astype(jnp.bfloat16).reshape(naux, nao, nao)
    moved = jnp.transpose(half_virt, (1, 0, 2)).reshape(nao, naux * nao)
    both_sides = jnp.dot(green_occ, moved, preferred_element_type=jnp.float32).astype(jnp.bfloat16)
    both_sides = jnp.transpose(both_sides.reshape(nao, naux, nao), (1, 0, 2)).reshape(naux, nao * nao)
    flat = screened.reshape(naux, nao * nao)
    return jnp.dot(both_sides, flat.T, preferred_element_type=jnp.float32)
```

```python
import jax
import jax.numpy as jnp
from jax import lax
from jax.sharding import PartitionSpec as P

BLK = 8


def gather_virt(green_virt):
    ranks = lax.axis_size("aux")
    me = lax.axis_index("aux")
    own = green_virt.T
    up = [(i, (i + 1) % ranks) for i in range(ranks)]
    down = [(i, (i - 1) % ranks) for i in range(ranks)]
    cols = own.shape[0]
    whole = jnp.zeros((ranks * cols, own.shape[1]), own.dtype)
    whole = lax.dynamic_update_slice_in_dim(whole, own, me * cols, 0)
    from_below, from_above = own, own
    for step in range(1, ranks // 2 + 1):
        from_below = lax.ppermute(from_below, "aux", up)
        whole = lax.dynamic_update_slice_in_dim(whole, from_below, lax.rem(me - step + ranks, ranks) * cols, 0)
        if 2 * step < ranks:
            from_above = lax.ppermute(from_above, "aux", down)
            whole = lax.dynamic_update_slice_in_dim(whole, from_above, lax.rem(me + step, ranks) * cols, 0)
    return whole


def shards(coulomb_blocks, occupancy, green_occ, green_virt):
    naux, mu_rows, nao = coulomb_blocks.shape
    ranks = lax.axis_size("orb")
    share = naux // lax.axis_size("aux")
    mask = jnp.repeat(jnp.repeat(occupancy, BLK, 0), BLK, 1).astype(jnp.bfloat16)
    own = lax.dynamic_slice_in_dim(coulomb_blocks, lax.axis_index("aux") * share, share, 0)
    screened = lax.all_to_all(own * mask[None], "orb", split_axis=0, concat_axis=0, tiled=True)
    screened = screened.reshape(nao, nao)
    virt_t = gather_virt(green_virt)
    half_virt = lax.dot_general(screened, virt_t, (((1,), (1,)), ((), ())), preferred_element_type=jnp.float32)
    both_sides = jnp.dot(green_occ, half_virt.astype(jnp.bfloat16), preferred_element_type=jnp.float32)
    both_sides = both_sides.astype(jnp.bfloat16).reshape(ranks, mu_rows, nao)
    returned = lax.all_to_all(both_sides, "orb", split_axis=0, concat_axis=0, tiled=True)
    partial_pol = jnp.einsum("qls,pls->qp", coulomb_blocks, returned * mask[None], preferred_element_type=jnp.float32)
    parts = lax.all_to_all(partial_pol, "orb", split_axis=0, concat_axis=0, tiled=True)
    return parts.reshape(ranks, naux // ranks, share).sum(0).T


def solution(mesh):
    in_specs = (P(None, "orb", None), P("orb", None), P(), P(None, "aux"))
    out_specs = P("aux", "orb")
    return jax.shard_map(shards, mesh=mesh, in_specs=in_specs, out_specs=out_specs, check_vma=False)
```

```python
import functools

import jax
import jax.numpy as jnp
from jax import lax
from jax.experimental import pallas as pl
from jax.experimental.pallas import tpu as pltpu
from jax.sharding import PartitionSpec as P

BLK = 8
LANES = 128
SCREEN_FLOPS = 1000
ALL_VMEM = 60 * 1024 * 1024
MOST_VMEM = 57 * 1024 * 1024
WIDE_VMEM = 10 * 1024 * 1024
PART = 64
SMALL_VMEM = 4 * 1024 * 1024
VMEM = pl.BlockSpec(memory_space=pltpu.VMEM)


def expand(occupancy, rows, cols):
    blocks = occupancy.shape[1]
    block = lax.broadcasted_iota(jnp.int32, (blocks, cols), 0)
    col = lax.broadcasted_iota(jnp.int32, (blocks, cols), 1)
    spread = (lax.div(col, BLK) == block).astype(jnp.float32)
    wide = jnp.dot(occupancy.astype(jnp.float32), spread, preferred_element_type=jnp.float32)
    return jnp.concatenate([jnp.broadcast_to(wide[i : i + 1], (BLK, cols)) for i in range(rows // BLK)], axis=0)


def screen_kernel(coulomb_ref, occupancy_ref, out_ref):
    rows, cols = coulomb_ref.shape[1:]
    mask = expand(occupancy_ref[...], rows, cols).astype(coulomb_ref.dtype)
    out_ref[...] = coulomb_ref[...] * mask[None]


def screen(coulomb_blocks, occupancy, share):
    rows, cols = coulomb_blocks.shape[1:]
    return pl.pallas_call(
        screen_kernel,
        grid=(1,),
        in_specs=[
            pl.BlockSpec((share, rows, cols), lambda i: (lax.axis_index("aux"), 0, 0)),
            pl.BlockSpec(occupancy.shape, lambda i: (0, 0)),
        ],
        out_specs=pl.BlockSpec((share, rows, cols), lambda i: (0, 0, 0)),
        out_shape=jax.ShapeDtypeStruct((share, rows, cols), coulomb_blocks.dtype),
        compiler_params=pltpu.CompilerParams(vmem_limit_bytes=ALL_VMEM),
        cost_estimate=pl.CostEstimate(flops=SCREEN_FLOPS, bytes_accessed=0, transcendentals=0),
        name="screen",
    )(coulomb_blocks, occupancy)


def fetch_virt(green_virt):
    ranks = lax.axis_size("aux")
    orbs = lax.axis_size("orb")
    own = green_virt.T
    half = own.shape[0] // 2
    own_half = lax.dynamic_slice_in_dim(own, lax.rem(lax.axis_index("orb"), 2) * half, half, 0)
    got = []
    for dist in range(1, ranks // 2 + 1):
        pairs = []
        for orb in range(orbs):
            for aux in range(ranks):
                target = (aux - dist if orb % 2 == 0 else aux + dist) % ranks
                pairs.append((orb * ranks + aux, orb * ranks + target))
        got.append(lax.ppermute(own if 2 * dist < ranks else own_half, ("orb", "aux"), pairs))
    return own, got


def swap_cores(blocks):
    pairs = [(i, i ^ 1) for i in range(lax.axis_size("orb"))]
    return [lax.ppermute(block, "orb", pairs) for block in blocks]


def assemble_kernel(ranks, own_ref, *refs):
    (*block_refs, out_ref) = refs
    me, side = lax.axis_index("aux"), lax.rem(lax.axis_index("orb"), 2)
    cols = own_ref.shape[0]
    far = ranks // 2
    out_ref[pl.ds(pl.multiple_of(me * cols, cols), cols), :] = own_ref[...]
    for which in range(2):
        core = side if which == 0 else 1 - side
        for dist in range(1, far + 1):
            ref = block_refs[which * far + dist - 1]
            source = lax.rem(me + ranks + jnp.where(core == 0, dist, -dist), ranks)
            first = source * cols + (core * (cols // 2) if 2 * dist == ranks else 0)
            out_ref[pl.ds(pl.multiple_of(first, cols // 2), ref.shape[0]), :] = ref[...]


def assemble(own, got, other):
    ranks = lax.axis_size("aux")
    blocks = [*got, *other]
    return pl.pallas_call(
        functools.partial(assemble_kernel, ranks),
        in_specs=[VMEM] * (1 + len(blocks)),
        out_specs=VMEM,
        out_shape=jax.ShapeDtypeStruct((ranks * own.shape[0], own.shape[1]), own.dtype),
        compiler_params=pltpu.CompilerParams(vmem_limit_bytes=SMALL_VMEM),
        name="assemble",
    )(own, *blocks)


def apply_virt_kernel(coulomb_ref, virt_ref, occupancy_ref, out_ref, mask):
    rows, count, cols = out_ref.shape

    @pl.when(pl.program_id(0) == 0)
    def _():
        once = expand(occupancy_ref[...], rows, cols)
        mask[...] = jnp.concatenate([once, once], axis=0).astype(mask.dtype)

    @pl.loop(0, count // PART)
    def _(i):
        here = pl.ds(pl.multiple_of(i * PART * rows, PART * rows), PART * rows)
        screened = coulomb_ref[here, :].reshape(PART // 2, 2 * rows, cols) * mask[...][None]
        half = jnp.dot(screened.reshape(PART * rows, cols), virt_ref[...], preferred_element_type=jnp.float32)
        half = half.reshape(PART, rows, cols).astype(out_ref.dtype)
        out_ref[:, pl.ds(pl.multiple_of(i * PART, PART), PART), :] = jnp.swapaxes(half, 0, 1)


def apply_virt(coulomb_blocks, virt_t, occupancy, count=64):
    naux, rows, cols = coulomb_blocks.shape
    dtype = coulomb_blocks.dtype
    return pl.pallas_call(
        apply_virt_kernel,
        grid=(naux // count,),
        in_specs=[
            pl.BlockSpec((count * rows, cols), lambda i: (i, 0)),
            pl.BlockSpec(virt_t.shape, lambda i: (0, 0)),
            pl.BlockSpec(occupancy.shape, lambda i: (0, 0)),
        ],
        out_specs=pl.BlockSpec((rows, count, cols), lambda i: (0, i, 0)),
        out_shape=jax.ShapeDtypeStruct((rows, naux, cols), dtype),
        scratch_shapes=[pltpu.VMEM((2 * rows, cols), dtype)],
        compiler_params=pltpu.CompilerParams(vmem_limit_bytes=ALL_VMEM),
        name="apply_virt",
    )(coulomb_blocks.reshape(naux * rows, cols), virt_t, occupancy)


def apply_occ_kernel(occ_ref, screened_ref, out_ref):
    out_ref[...] = jnp.dot(occ_ref[...], screened_ref[...], preferred_element_type=jnp.float32).astype(out_ref.dtype)


def apply_occ(green_occ, screened):
    return pl.pallas_call(
        apply_occ_kernel,
        in_specs=[VMEM] * 2,
        out_specs=VMEM,
        out_shape=jax.ShapeDtypeStruct(screened.shape, screened.dtype),
        compiler_params=pltpu.CompilerParams(vmem_limit_bytes=WIDE_VMEM),
        name="apply_occ",
    )(green_occ, screened)


def contract_kernel(returned_ref, half_ref, out_ref, left, right, sem):
    rows, naux, cols = left.shape
    share = right.shape[1]
    chunks = sem.shape[0]
    depth = rows // chunks

    def fetch(i):
        here = pl.ds(i * depth, depth)
        return pltpu.make_async_copy(half_ref.at[here], left.at[here], sem.at[i])

    for i in range(chunks):
        fetch(i).start()

    @pl.loop(0, share // 16)
    def _(i):
        here = pl.ds(pl.multiple_of(i * 16, 16), 16)
        right[:, here, :] = jnp.swapaxes(returned_ref[here], 0, 1)

    out_ref[...] = jnp.zeros(out_ref.shape, out_ref.dtype)

    @pl.loop(0, chunks)
    def _(i):
        fetch(i).wait()
        total = jnp.zeros((naux, share), jnp.float32)
        for j in range(depth):
            total += lax.dot_general(
                left[i * depth + j], right[i * depth + j], (((1,), (1,)), ((), ())), preferred_element_type=jnp.float32
            )
        out_ref[:, :share] += total


def contract(half_rows, returned, chunks=4):
    rows, naux, cols = half_rows.shape
    share = returned.shape[0]
    dtype = half_rows.dtype
    return pl.pallas_call(
        contract_kernel,
        in_specs=[VMEM, pl.BlockSpec(memory_space=pl.ANY)],
        out_specs=VMEM,
        out_shape=jax.ShapeDtypeStruct((naux, LANES), jnp.float32),
        scratch_shapes=[
            pltpu.VMEM((rows, naux, cols), dtype),
            pltpu.VMEM((rows, share, cols), dtype),
            pltpu.SemaphoreType.DMA((chunks,)),
        ],
        compiler_params=pltpu.CompilerParams(vmem_limit_bytes=MOST_VMEM),
        name="contract",
    )(returned, half_rows)


def finish_kernel(parts_ref, out_ref):
    out_ref[...] = jnp.sum(parts_ref[...], axis=0)[:, : out_ref.shape[1]]


def finish(parts, share):
    return pl.pallas_call(
        finish_kernel,
        in_specs=[VMEM],
        out_specs=pl.BlockSpec((parts.shape[1], share), lambda: (0, 0)),
        out_shape=jax.ShapeDtypeStruct((parts.shape[1], share), parts.dtype),
        name="finish",
    )(parts)


def shards(coulomb_blocks, occupancy, green_occ, green_virt):
    naux, mu_rows, nao = coulomb_blocks.shape
    ranks = lax.axis_size("orb")
    planes = lax.axis_size("aux")
    share = naux // planes
    own = screen(coulomb_blocks, occupancy, share)
    own_virt, got = fetch_virt(green_virt)
    screened = lax.all_to_all(own, "orb", split_axis=0, concat_axis=0, tiled=True).reshape(nao, nao)
    half_occ = apply_occ(green_occ, screened)
    half_occ, *got = lax.optimization_barrier((half_occ, *got))
    virt_t = assemble(own_virt, got, swap_cores(got))
    half_rows = apply_virt(coulomb_blocks, virt_t, occupancy)
    returned = lax.all_to_all(half_occ.reshape(ranks, mu_rows, nao), "orb", split_axis=0, concat_axis=0, tiled=True)
    partial_pol = contract(half_rows, returned)
    parts = partial_pol.reshape(ranks, naux // ranks, LANES)
    parts = lax.all_to_all(parts, "orb", split_axis=0, concat_axis=0, tiled=True)
    return finish(parts, share).T


def solution(mesh):
    in_specs = (P(None, "orb", None), P("orb", None), P(), P(None, "aux"))
    out_specs = P("aux", "orb")
    return jax.shard_map(shards, mesh=mesh, in_specs=in_specs, out_specs=out_specs, check_vma=False)
```

```python
import functools

import jax
import jax.numpy as jnp
from jax import lax
from jax.experimental import pallas as pl
from jax.experimental.pallas import tpu as pltpu
from jax.sharding import PartitionSpec as P

BLK = 8
LANES = 128
SCREEN_FLOPS = 1000
ALL_VMEM = 60 * 1024 * 1024
MOST_VMEM = 48 * 1024 * 1024
WIDE_VMEM = 10 * 1024 * 1024
PART = 64
SMALL_VMEM = 4 * 1024 * 1024
VMEM = pl.BlockSpec(memory_space=pltpu.VMEM)
ANY = pl.BlockSpec(memory_space=pl.ANY)


def expand(occupancy, rows, cols):
    blocks = occupancy.shape[1]
    block = lax.broadcasted_iota(jnp.int32, (blocks, cols), 0)
    col = lax.broadcasted_iota(jnp.int32, (blocks, cols), 1)
    spread = (lax.div(col, BLK) == block).astype(jnp.float32)
    wide = jnp.dot(occupancy.astype(jnp.float32), spread, preferred_element_type=jnp.float32)
    return jnp.concatenate([jnp.broadcast_to(wide[i : i + 1], (BLK, cols)) for i in range(rows // BLK)], axis=0)


def screen_kernel(coulomb_ref, occupancy_ref, out_ref, part, occupancy, in_sem, out_sem, occupancy_sem):
    share, rows, cols = part.shape
    chunks = in_sem.shape[0]
    block = share // chunks
    first = lax.axis_index("aux") * share

    def fetch(i):
        return pltpu.make_async_copy(
            coulomb_ref.at[pl.ds(first + i * block, block)], part.at[pl.ds(i * block, block)], in_sem.at[i]
        )

    def put(i):
        here = pl.ds(i * block, block)
        return pltpu.make_async_copy(part.at[here], out_ref.at[here], out_sem.at[i])

    copy = pltpu.make_async_copy(occupancy_ref, occupancy, occupancy_sem)
    copy.start()
    for i in range(chunks):
        fetch(i).start()
    copy.wait()
    mask = expand(occupancy[...], rows, cols).astype(part.dtype)

    @pl.loop(0, chunks)
    def _(i):
        fetch(i).wait()
        here = pl.ds(i * block, block)
        part[here] = part[here] * mask[None]
        put(i).start()

    @pl.loop(0, chunks)
    def _(i):
        put(i).wait()


def screen(coulomb_blocks, occupancy, share, chunks=4):
    part = (share, *coulomb_blocks.shape[1:])
    dtype = coulomb_blocks.dtype
    return pl.pallas_call(
        screen_kernel,
        in_specs=[ANY, ANY],
        out_specs=ANY,
        out_shape=jax.ShapeDtypeStruct(part, dtype),
        scratch_shapes=[
            pltpu.VMEM(part, dtype),
            pltpu.VMEM(occupancy.shape, occupancy.dtype),
            pltpu.SemaphoreType.DMA((chunks,)),
            pltpu.SemaphoreType.DMA((chunks,)),
            pltpu.SemaphoreType.DMA,
        ],
        compiler_params=pltpu.CompilerParams(vmem_limit_bytes=ALL_VMEM),
        name="screen",
    )(coulomb_blocks, occupancy)


def fetch_virt(green_virt):
    ranks = lax.axis_size("aux")
    orbs = lax.axis_size("orb")
    own = green_virt.T
    half = own.shape[0] // 2
    own_half = lax.dynamic_slice_in_dim(own, lax.rem(lax.axis_index("orb"), 2) * half, half, 0)
    got = []
    for dist in range(1, ranks // 2 + 1):
        pairs = []
        for orb in range(orbs):
            for aux in range(ranks):
                target = (aux - dist if orb % 2 == 0 else aux + dist) % ranks
                pairs.append((orb * ranks + aux, orb * ranks + target))
        got.append(lax.ppermute(own if 2 * dist < ranks else own_half, ("orb", "aux"), pairs))
    return own, got


def swap_cores(blocks):
    pairs = [(i, i ^ 1) for i in range(lax.axis_size("orb"))]
    return [lax.ppermute(block, "orb", pairs) for block in blocks]


def assemble_kernel(ranks, own_ref, *refs):
    (*block_refs, out_ref) = refs
    me, side = lax.axis_index("aux"), lax.rem(lax.axis_index("orb"), 2)
    cols = own_ref.shape[0]
    far = ranks // 2
    out_ref[pl.ds(pl.multiple_of(me * cols, cols), cols), :] = own_ref[...]
    for which in range(2):
        core = side if which == 0 else 1 - side
        for dist in range(1, far + 1):
            ref = block_refs[which * far + dist - 1]
            source = lax.rem(me + ranks + jnp.where(core == 0, dist, -dist), ranks)
            first = source * cols + (core * (cols // 2) if 2 * dist == ranks else 0)
            out_ref[pl.ds(pl.multiple_of(first, cols // 2), ref.shape[0]), :] = ref[...]


def assemble(own, got, other):
    ranks = lax.axis_size("aux")
    blocks = [*got, *other]
    return pl.pallas_call(
        functools.partial(assemble_kernel, ranks),
        in_specs=[VMEM] * (1 + len(blocks)),
        out_specs=VMEM,
        out_shape=jax.ShapeDtypeStruct((ranks * own.shape[0], own.shape[1]), own.dtype),
        compiler_params=pltpu.CompilerParams(vmem_limit_bytes=SMALL_VMEM),
        name="assemble",
    )(own, *blocks)


def apply_virt_kernel(coulomb_ref, virt_ref, occupancy_ref, out_ref, mask):
    rows, count, cols = out_ref.shape

    @pl.when(pl.program_id(0) == 0)
    def _():
        once = expand(occupancy_ref[...], rows, cols)
        mask[...] = jnp.concatenate([once, once], axis=0).astype(mask.dtype)

    @pl.loop(0, count // PART)
    def _(i):
        here = pl.ds(pl.multiple_of(i * PART * rows, PART * rows), PART * rows)
        screened = coulomb_ref[here, :].reshape(PART // 2, 2 * rows, cols) * mask[...][None]
        half = jnp.dot(screened.reshape(PART * rows, cols), virt_ref[...], preferred_element_type=jnp.float32)
        half = half.reshape(PART, rows, cols).astype(out_ref.dtype)
        out_ref[:, pl.ds(pl.multiple_of(i * PART, PART), PART), :] = jnp.swapaxes(half, 0, 1)


def apply_virt(coulomb_blocks, virt_t, occupancy, count=64):
    naux, rows, cols = coulomb_blocks.shape
    dtype = coulomb_blocks.dtype
    return pl.pallas_call(
        apply_virt_kernel,
        grid=(naux // count,),
        in_specs=[
            pl.BlockSpec((count * rows, cols), lambda i: (i, 0)),
            pl.BlockSpec(virt_t.shape, lambda i: (0, 0)),
            pl.BlockSpec(occupancy.shape, lambda i: (0, 0)),
        ],
        out_specs=pl.BlockSpec((rows, count, cols), lambda i: (0, i, 0)),
        out_shape=jax.ShapeDtypeStruct((2 * rows, naux, cols), dtype),
        scratch_shapes=[pltpu.VMEM((2 * rows, cols), dtype)],
        compiler_params=pltpu.CompilerParams(vmem_limit_bytes=ALL_VMEM),
        name="apply_virt",
    )(coulomb_blocks.reshape(naux * rows, cols), virt_t, occupancy)


def apply_occ_kernel(occ_ref, screened_ref, out_ref, half, sem):
    chunks = sem.shape[0]
    block = half.shape[0] // chunks
    copies = []
    for i in range(chunks):
        here = pl.ds(i * block, block)
        half[here, :] = jnp.dot(
            occ_ref[here, :], screened_ref[...], preferred_element_type=jnp.float32
        ).astype(half.dtype)
        copies.append(pltpu.make_async_copy(half.at[here], out_ref.at[here], sem.at[i]))
        copies[-1].start()
    for copy in copies:
        copy.wait()


def apply_occ(green_occ, screened, chunks=3):
    return pl.pallas_call(
        apply_occ_kernel,
        in_specs=[VMEM] * 2,
        out_specs=ANY,
        out_shape=jax.ShapeDtypeStruct(screened.shape, screened.dtype),
        scratch_shapes=[pltpu.VMEM(screened.shape, screened.dtype), pltpu.SemaphoreType.DMA((chunks,))],
        compiler_params=pltpu.CompilerParams(vmem_limit_bytes=WIDE_VMEM),
        name="apply_occ",
    )(green_occ, screened)


def contract_kernel(returned_ref, half_ref, out_ref, left, right, sem):
    rows, naux, cols = left.shape
    share = right.shape[1]
    chunks = sem.shape[0]
    depth = rows // chunks

    def fetch(i):
        here = pl.ds(i * depth, depth)
        return pltpu.make_async_copy(half_ref.at[here], left.at[here], sem.at[i])

    for i in range(chunks):
        fetch(i).start()

    @pl.loop(0, share // 16)
    def _(i):
        here = pl.ds(pl.multiple_of(i * 16, 16), 16)
        right[:, here, :] = jnp.swapaxes(returned_ref[here], 0, 1)

    out_ref[...] = jnp.zeros(out_ref.shape, out_ref.dtype)

    @pl.loop(0, chunks)
    def _(i):
        fetch(i).wait()
        total = jnp.zeros((naux, share), jnp.float32)
        for j in range(depth):
            total += lax.dot_general(
                left[i * depth + j], right[i * depth + j], (((1,), (1,)), ((), ())), preferred_element_type=jnp.float32
            )
        out_ref[:, :share] += total


def contract(half_rows, returned, chunks=4):
    _, naux, cols = half_rows.shape
    share, rows, _ = returned.shape
    dtype = half_rows.dtype
    return pl.pallas_call(
        contract_kernel,
        in_specs=[VMEM, ANY],
        out_specs=VMEM,
        out_shape=jax.ShapeDtypeStruct((naux, LANES), jnp.float32),
        scratch_shapes=[
            pltpu.VMEM((rows, naux, cols), dtype),
            pltpu.VMEM((rows, share, cols), dtype),
            pltpu.SemaphoreType.DMA((chunks,)),
        ],
        compiler_params=pltpu.CompilerParams(vmem_limit_bytes=MOST_VMEM),
        name="contract",
    )(returned, half_rows)


def finish(parts, share):
    return jnp.sum(parts[:, :, :share], axis=0)


def shards(coulomb_blocks, occupancy, green_occ, green_virt):
    naux, mu_rows, nao = coulomb_blocks.shape
    ranks = lax.axis_size("orb")
    planes = lax.axis_size("aux")
    share = naux // planes
    own = screen(coulomb_blocks, occupancy, share)
    own_virt, got = fetch_virt(green_virt)
    screened = lax.all_to_all(own, "orb", split_axis=0, concat_axis=0, tiled=True).reshape(nao, nao)
    half_occ = apply_occ(green_occ, screened)
    half_occ, *got = lax.optimization_barrier((half_occ, *got))
    virt_t = assemble(own_virt, got, swap_cores(got))
    half_rows = apply_virt(coulomb_blocks, virt_t, occupancy)
    returned = lax.all_to_all(half_occ.reshape(ranks, mu_rows, nao), "orb", split_axis=0, concat_axis=0, tiled=True)
    partial_pol = contract(half_rows, returned)
    parts = partial_pol.reshape(ranks, naux // ranks, LANES)
    parts = lax.all_to_all(parts, "orb", split_axis=0, concat_axis=0, tiled=True)
    return finish(parts, share).T


def solution(mesh):
    in_specs = (P(None, "orb", None), P("orb", None), P(), P(None, "aux"))
    out_specs = P("aux", "orb")
    return jax.shard_map(shards, mesh=mesh, in_specs=in_specs, out_specs=out_specs, check_vma=False)
```

```python
import functools

import jax
import jax.numpy as jnp
from jax import lax
from jax.experimental import pallas as pl
from jax.experimental.pallas import tpu as pltpu
from jax.sharding import PartitionSpec as P

BLK = 8
LANES = 128
SCREEN_FLOPS = 1000
ALL_VMEM = 60 * 1024 * 1024
MOST_VMEM = 48 * 1024 * 1024
WIDE_VMEM = 10 * 1024 * 1024
PART = 64
PRODUCT_VMEM = 56 * 1024 * 1024
VMEM = pl.BlockSpec(memory_space=pltpu.VMEM)
ANY = pl.BlockSpec(memory_space=pl.ANY)


def expand(occupancy, rows, cols):
    blocks = occupancy.shape[1]
    block = lax.broadcasted_iota(jnp.int32, (blocks, cols), 0)
    col = lax.broadcasted_iota(jnp.int32, (blocks, cols), 1)
    spread = (lax.div(col, BLK) == block).astype(jnp.float32)
    wide = jnp.dot(occupancy.astype(jnp.float32), spread, preferred_element_type=jnp.float32)
    return jnp.concatenate([jnp.broadcast_to(wide[i : i + 1], (BLK, cols)) for i in range(rows // BLK)], axis=0)


def screen_kernel(coulomb_ref, occupancy_ref, out_ref, part, occupancy, in_sem, out_sem, occupancy_sem):
    share, rows, cols = part.shape
    chunks = in_sem.shape[0]
    block = share // chunks
    first = lax.axis_index("aux") * share

    def fetch(i):
        return pltpu.make_async_copy(
            coulomb_ref.at[pl.ds(first + i * block, block)], part.at[pl.ds(i * block, block)], in_sem.at[i]
        )

    def put(i):
        here = pl.ds(i * block, block)
        return pltpu.make_async_copy(part.at[here], out_ref.at[here], out_sem.at[i])

    copy = pltpu.make_async_copy(occupancy_ref, occupancy, occupancy_sem)
    copy.start()
    for i in range(chunks):
        fetch(i).start()
    copy.wait()
    mask = expand(occupancy[...], rows, cols).astype(part.dtype)

    @pl.loop(0, chunks)
    def _(i):
        fetch(i).wait()
        here = pl.ds(i * block, block)
        part[here] = part[here] * mask[None]
        put(i).start()

    @pl.loop(0, chunks)
    def _(i):
        put(i).wait()


def screen(coulomb_blocks, occupancy, share, chunks=4):
    part = (share, *coulomb_blocks.shape[1:])
    dtype = coulomb_blocks.dtype
    return pl.pallas_call(
        screen_kernel,
        in_specs=[ANY, ANY],
        out_specs=ANY,
        out_shape=jax.ShapeDtypeStruct(part, dtype),
        scratch_shapes=[
            pltpu.VMEM(part, dtype),
            pltpu.VMEM(occupancy.shape, occupancy.dtype),
            pltpu.SemaphoreType.DMA((chunks,)),
            pltpu.SemaphoreType.DMA((chunks,)),
            pltpu.SemaphoreType.DMA,
        ],
        compiler_params=pltpu.CompilerParams(vmem_limit_bytes=ALL_VMEM),
        name="screen",
    )(coulomb_blocks, occupancy)


def fetch_virt(green_virt):
    ranks = lax.axis_size("aux")
    orbs = lax.axis_size("orb")
    own = green_virt.T
    half = own.shape[0] // 2
    own_half = lax.dynamic_slice_in_dim(own, lax.rem(lax.axis_index("orb"), 2) * half, half, 0)
    got = {}
    for dist in range(ranks // 2, 0, -1):
        pairs = []
        for orb in range(orbs):
            for aux in range(ranks):
                target = (aux - dist if orb % 2 == 0 else aux + dist) % ranks
                pairs.append((orb * ranks + aux, orb * ranks + target))
        got[dist] = lax.ppermute(own if 2 * dist < ranks else own_half, ("orb", "aux"), pairs)
    return own, [got[dist] for dist in sorted(got)]


def swap_cores(blocks):
    pairs = [(i, i ^ 1) for i in range(lax.axis_size("orb"))]
    return [lax.ppermute(block, "orb", pairs) for block in blocks]


def assemble(ranks, own_ref, block_refs, virt):
    me, side = lax.axis_index("aux"), lax.rem(lax.axis_index("orb"), 2)
    cols = own_ref.shape[0]
    far = ranks // 2
    virt[pl.ds(pl.multiple_of(me * cols, cols), cols), :] = own_ref[...]
    for which in range(2):
        core = side if which == 0 else 1 - side
        for dist in range(1, far + 1):
            ref = block_refs[which * far + dist - 1]
            source = lax.rem(me + ranks + jnp.where(core == 0, dist, -dist), ranks)
            first = source * cols + (core * (cols // 2) if 2 * dist == ranks else 0)
            virt[pl.ds(pl.multiple_of(first, cols // 2), ref.shape[0]), :] = ref[...]


def apply_virt_kernel(ranks, coulomb_ref, occupancy_ref, own_ref, *refs):
    (*block_refs, out_ref, virt, mask) = refs
    rows, count, cols = out_ref.shape

    @pl.when(pl.program_id(0) == 0)
    def _():
        once = expand(occupancy_ref[...], rows, cols)
        mask[...] = jnp.concatenate([once, once], axis=0).astype(mask.dtype)
        assemble(ranks, own_ref, block_refs, virt)

    @pl.loop(0, count // PART)
    def _(i):
        here = pl.ds(pl.multiple_of(i * PART * rows, PART * rows), PART * rows)
        screened = coulomb_ref[here, :].reshape(PART // 2, 2 * rows, cols) * mask[...][None]
        half = jnp.dot(screened.reshape(PART * rows, cols), virt[...], preferred_element_type=jnp.float32)
        half = half.reshape(PART, rows, cols).astype(out_ref.dtype)
        out_ref[:, pl.ds(pl.multiple_of(i * PART, PART), PART), :] = jnp.swapaxes(half, 0, 1)


def apply_virt(coulomb_blocks, occupancy, own, blocks, count=64):
    naux, rows, cols = coulomb_blocks.shape
    dtype = coulomb_blocks.dtype
    ranks = lax.axis_size("aux")
    return pl.pallas_call(
        functools.partial(apply_virt_kernel, ranks),
        grid=(naux // count,),
        in_specs=[
            pl.BlockSpec((count * rows, cols), lambda i: (i, 0)),
            pl.BlockSpec(occupancy.shape, lambda i: (0, 0)),
            *[VMEM] * (1 + len(blocks)),
        ],
        out_specs=pl.BlockSpec((rows, count, cols), lambda i: (0, i, 0)),
        out_shape=jax.ShapeDtypeStruct((2 * rows, naux, cols), dtype),
        scratch_shapes=[pltpu.VMEM((ranks * own.shape[0], cols), dtype), pltpu.VMEM((2 * rows, cols), dtype)],
        compiler_params=pltpu.CompilerParams(vmem_limit_bytes=PRODUCT_VMEM),
        name="apply_virt",
    )(coulomb_blocks.reshape(naux * rows, cols), occupancy, own, *blocks)


def apply_occ_kernel(occ_ref, screened_ref, out_ref, half, sem):
    chunks = sem.shape[0]
    block = half.shape[0] // chunks
    copies = []
    for i in range(chunks):
        here = pl.ds(i * block, block)
        half[here, :] = jnp.dot(
            occ_ref[here, :], screened_ref[...], preferred_element_type=jnp.float32
        ).astype(half.dtype)
        copies.append(pltpu.make_async_copy(half.at[here], out_ref.at[here], sem.at[i]))
        copies[-1].start()
    for copy in copies:
        copy.wait()


def apply_occ(green_occ, screened, chunks=3):
    return pl.pallas_call(
        apply_occ_kernel,
        in_specs=[VMEM] * 2,
        out_specs=ANY,
        out_shape=jax.ShapeDtypeStruct(screened.shape, screened.dtype),
        scratch_shapes=[pltpu.VMEM(screened.shape, screened.dtype), pltpu.SemaphoreType.DMA((chunks,))],
        compiler_params=pltpu.CompilerParams(vmem_limit_bytes=WIDE_VMEM),
        name="apply_occ",
    )(green_occ, screened)


def contract_kernel(returned_ref, half_ref, out_ref, left, right, sem):
    rows, naux, cols = left.shape
    share = right.shape[1]
    chunks = sem.shape[0]
    depth = rows // chunks

    def fetch(i):
        here = pl.ds(i * depth, depth)
        return pltpu.make_async_copy(half_ref.at[here], left.at[here], sem.at[i])

    for i in range(chunks):
        fetch(i).start()

    @pl.loop(0, share // 16)
    def _(i):
        here = pl.ds(pl.multiple_of(i * 16, 16), 16)
        right[:, here, :] = jnp.swapaxes(returned_ref[here], 0, 1)

    out_ref[...] = jnp.zeros(out_ref.shape, out_ref.dtype)

    @pl.loop(0, chunks)
    def _(i):
        fetch(i).wait()
        total = jnp.zeros((naux, share), jnp.float32)
        for j in range(depth):
            total += lax.dot_general(
                left[i * depth + j], right[i * depth + j], (((1,), (1,)), ((), ())), preferred_element_type=jnp.float32
            )
        out_ref[:, :share] += total


def contract(half_rows, returned, chunks=4):
    _, naux, cols = half_rows.shape
    share, rows, _ = returned.shape
    dtype = half_rows.dtype
    return pl.pallas_call(
        contract_kernel,
        in_specs=[VMEM, ANY],
        out_specs=VMEM,
        out_shape=jax.ShapeDtypeStruct((naux, LANES), jnp.float32),
        scratch_shapes=[
            pltpu.VMEM((rows, naux, cols), dtype),
            pltpu.VMEM((rows, share, cols), dtype),
            pltpu.SemaphoreType.DMA((chunks,)),
        ],
        compiler_params=pltpu.CompilerParams(vmem_limit_bytes=MOST_VMEM),
        name="contract",
    )(returned, half_rows)


def finish(parts, share):
    return jnp.sum(parts[:, :, :share], axis=0)


def shards(coulomb_blocks, occupancy, green_occ, green_virt):
    naux, mu_rows, nao = coulomb_blocks.shape
    ranks = lax.axis_size("orb")
    planes = lax.axis_size("aux")
    share = naux // planes
    own = screen(coulomb_blocks, occupancy, share)
    own_virt, got = fetch_virt(green_virt)
    screened = lax.all_to_all(own, "orb", split_axis=0, concat_axis=0, tiled=True).reshape(nao, nao)
    half_occ = apply_occ(green_occ, screened)
    half_occ, *late = lax.optimization_barrier((half_occ, *got))
    half_rows = apply_virt(coulomb_blocks, occupancy, own_virt, [*late, *swap_cores(late)])
    returned = lax.all_to_all(half_occ.reshape(ranks, mu_rows, nao), "orb", split_axis=0, concat_axis=0, tiled=True)
    partial_pol = contract(half_rows, returned)
    parts = partial_pol.reshape(ranks, naux // ranks, LANES)
    parts = lax.all_to_all(parts, "orb", split_axis=0, concat_axis=0, tiled=True)
    return finish(parts, share).T


def solution(mesh):
    in_specs = (P(None, "orb", None), P("orb", None), P(), P(None, "aux"))
    out_specs = P("aux", "orb")
    return jax.shard_map(shards, mesh=mesh, in_specs=in_specs, out_specs=out_specs, check_vma=False)
```

```python
import functools

import jax
import jax.numpy as jnp
from jax import lax
from jax.experimental import pallas as pl
from jax.experimental.pallas import tpu as pltpu
from jax.sharding import PartitionSpec as P

BLK = 8
LANES = 128
SCREEN_FLOPS = 1000
ALL_VMEM = 60 * 1024 * 1024
MOST_VMEM = 48 * 1024 * 1024
WIDE_VMEM = 10 * 1024 * 1024
PART = 64
PRODUCT_VMEM = 56 * 1024 * 1024
VMEM = pl.BlockSpec(memory_space=pltpu.VMEM)
ANY = pl.BlockSpec(memory_space=pl.ANY)


def expand(occupancy, rows, cols):
    blocks = occupancy.shape[1]
    block = lax.broadcasted_iota(jnp.int32, (blocks, cols), 0)
    col = lax.broadcasted_iota(jnp.int32, (blocks, cols), 1)
    spread = (lax.div(col, BLK) == block).astype(jnp.float32)
    wide = jnp.dot(occupancy.astype(jnp.float32), spread, preferred_element_type=jnp.float32)
    return jnp.concatenate([jnp.broadcast_to(wide[i : i + 1], (BLK, cols)) for i in range(rows // BLK)], axis=0)


def screen_kernel(coulomb_ref, occupancy_ref, out_ref, part, occupancy, in_sem, out_sem, occupancy_sem):
    share, rows, cols = part.shape
    chunks = in_sem.shape[0]
    block = share // chunks
    first = lax.axis_index("aux") * share

    def fetch(i):
        return pltpu.make_async_copy(
            coulomb_ref.at[pl.ds(first + i * block, block)], part.at[pl.ds(i * block, block)], in_sem.at[i]
        )

    def put(i):
        here = pl.ds(i * block, block)
        return pltpu.make_async_copy(part.at[here], out_ref.at[here], out_sem.at[i])

    copy = pltpu.make_async_copy(occupancy_ref, occupancy, occupancy_sem)
    copy.start()
    for i in range(chunks):
        fetch(i).start()
    copy.wait()
    mask = expand(occupancy[...], rows, cols).astype(part.dtype)

    @pl.loop(0, chunks)
    def _(i):
        fetch(i).wait()
        here = pl.ds(i * block, block)
        part[here] = part[here] * mask[None]
        put(i).start()

    @pl.loop(0, chunks)
    def _(i):
        put(i).wait()


def screen(coulomb_blocks, occupancy, share, chunks=4):
    part = (share, *coulomb_blocks.shape[1:])
    dtype = coulomb_blocks.dtype
    return pl.pallas_call(
        screen_kernel,
        in_specs=[ANY, ANY],
        out_specs=ANY,
        out_shape=jax.ShapeDtypeStruct(part, dtype),
        scratch_shapes=[
            pltpu.VMEM(part, dtype),
            pltpu.VMEM(occupancy.shape, occupancy.dtype),
            pltpu.SemaphoreType.DMA((chunks,)),
            pltpu.SemaphoreType.DMA((chunks,)),
            pltpu.SemaphoreType.DMA,
        ],
        compiler_params=pltpu.CompilerParams(vmem_limit_bytes=ALL_VMEM),
        name="screen",
    )(coulomb_blocks, occupancy)


def fetch_virt(green_virt):
    ranks = lax.axis_size("aux")
    orbs = lax.axis_size("orb")
    own = green_virt.T
    half = own.shape[0] // 2
    own_half = lax.dynamic_slice_in_dim(own, lax.rem(lax.axis_index("orb"), 2) * half, half, 0)
    got = {}
    for dist in range(ranks // 2, 0, -1):
        pairs = []
        for orb in range(orbs):
            for aux in range(ranks):
                target = (aux - dist if orb % 2 == 0 else aux + dist) % ranks
                pairs.append((orb * ranks + aux, orb * ranks + target))
        got[dist] = lax.ppermute(own if 2 * dist < ranks else own_half, ("orb", "aux"), pairs)
    return own, [got[dist] for dist in sorted(got)]


def swap_cores(blocks):
    pairs = [(i, i ^ 1) for i in range(lax.axis_size("orb"))]
    return [lax.ppermute(block, "orb", pairs) for block in blocks]


def assemble(ranks, own_ref, block_refs, virt):
    me, side = lax.axis_index("aux"), lax.rem(lax.axis_index("orb"), 2)
    cols = own_ref.shape[0]
    far = ranks // 2
    virt[pl.ds(pl.multiple_of(me * cols, cols), cols), :] = own_ref[...]
    for which in range(2):
        core = side if which == 0 else 1 - side
        for dist in range(1, far + 1):
            ref = block_refs[which * far + dist - 1]
            source = lax.rem(me + ranks + jnp.where(core == 0, dist, -dist), ranks)
            first = source * cols + (core * (cols // 2) if 2 * dist == ranks else 0)
            virt[pl.ds(pl.multiple_of(first, cols // 2), ref.shape[0]), :] = ref[...]


def apply_virt_kernel(ranks, coulomb_ref, occupancy_ref, own_ref, *refs):
    (*block_refs, out_ref, virt, mask) = refs
    rows, count, cols = out_ref.shape

    @pl.when(pl.program_id(0) == 0)
    def _():
        once = expand(occupancy_ref[...], rows, cols)
        mask[...] = jnp.concatenate([once, once], axis=0).astype(mask.dtype)
        assemble(ranks, own_ref, block_refs, virt)

    @pl.loop(0, count // PART)
    def _(i):
        here = pl.ds(pl.multiple_of(i * PART * rows, PART * rows), PART * rows)
        screened = coulomb_ref[here, :].reshape(PART // 2, 2 * rows, cols) * mask[...][None]
        half = jnp.dot(screened.reshape(PART * rows, cols), virt[...], preferred_element_type=jnp.float32)
        half = half.reshape(PART, rows, cols).astype(out_ref.dtype)
        out_ref[:, pl.ds(pl.multiple_of(i * PART, PART), PART), :] = jnp.swapaxes(half, 0, 1)


def apply_virt(coulomb_blocks, occupancy, own, blocks, count=64):
    naux, rows, cols = coulomb_blocks.shape
    dtype = coulomb_blocks.dtype
    ranks = lax.axis_size("aux")
    return pl.pallas_call(
        functools.partial(apply_virt_kernel, ranks),
        grid=(naux // count,),
        in_specs=[
            pl.BlockSpec((count * rows, cols), lambda i: (i, 0)),
            pl.BlockSpec(occupancy.shape, lambda i: (0, 0)),
            *[VMEM] * (1 + len(blocks)),
        ],
        out_specs=pl.BlockSpec((rows, count, cols), lambda i: (0, i, 0)),
        out_shape=jax.ShapeDtypeStruct((2 * rows, naux, cols), dtype),
        scratch_shapes=[pltpu.VMEM((ranks * own.shape[0], cols), dtype), pltpu.VMEM((2 * rows, cols), dtype)],
        compiler_params=pltpu.CompilerParams(vmem_limit_bytes=PRODUCT_VMEM),
        name="apply_virt",
    )(coulomb_blocks.reshape(naux * rows, cols), occupancy, own, *blocks)


def apply_occ_kernel(occ_ref, screened_ref, out_ref, half, sem):
    chunks = sem.shape[0]
    block = half.shape[0] // chunks
    copies = []
    for i in range(chunks):
        here = pl.ds(i * block, block)
        half[here, :] = jnp.dot(
            occ_ref[here, :], screened_ref[...], preferred_element_type=jnp.float32
        ).astype(half.dtype)
        copies.append(pltpu.make_async_copy(half.at[here], out_ref.at[here], sem.at[i]))
        copies[-1].start()
    for copy in copies:
        copy.wait()


def apply_occ(green_occ, screened, chunks=2):
    return pl.pallas_call(
        apply_occ_kernel,
        in_specs=[VMEM] * 2,
        out_specs=ANY,
        out_shape=jax.ShapeDtypeStruct(screened.shape, screened.dtype),
        scratch_shapes=[pltpu.VMEM(screened.shape, screened.dtype), pltpu.SemaphoreType.DMA((chunks,))],
        compiler_params=pltpu.CompilerParams(vmem_limit_bytes=WIDE_VMEM),
        name="apply_occ",
    )(green_occ, screened)


def contract_kernel(returned_ref, half_ref, out_ref, left, right, sem):
    rows, naux, cols = left.shape
    share = right.shape[1]
    chunks = sem.shape[0]
    depth = rows // chunks

    def fetch(i):
        here = pl.ds(i * depth, depth)
        return pltpu.make_async_copy(half_ref.at[here], left.at[here], sem.at[i])

    for i in range(chunks):
        fetch(i).start()

    @pl.loop(0, share // 16)
    def _(i):
        here = pl.ds(pl.multiple_of(i * 16, 16), 16)
        right[:, here, :] = jnp.swapaxes(returned_ref[here], 0, 1)

    out_ref[...] = jnp.zeros(out_ref.shape, out_ref.dtype)

    @pl.loop(0, chunks)
    def _(i):
        fetch(i).wait()
        total = jnp.zeros((naux, share), jnp.float32)
        for j in range(depth):
            total += lax.dot_general(
                left[i * depth + j], right[i * depth + j], (((1,), (1,)), ((), ())), preferred_element_type=jnp.float32
            )
        out_ref[:, :share] += total


def contract(half_rows, returned, chunks=6):
    _, naux, cols = half_rows.shape
    share, rows, _ = returned.shape
    dtype = half_rows.dtype
    return pl.pallas_call(
        contract_kernel,
        in_specs=[VMEM, ANY],
        out_specs=VMEM,
        out_shape=jax.ShapeDtypeStruct((naux, LANES), jnp.float32),
        scratch_shapes=[
            pltpu.VMEM((rows, naux, cols), dtype),
            pltpu.VMEM((rows, share, cols), dtype),
            pltpu.SemaphoreType.DMA((chunks,)),
        ],
        compiler_params=pltpu.CompilerParams(vmem_limit_bytes=MOST_VMEM),
        name="contract",
    )(returned, half_rows)


def finish(parts, share):
    return jnp.sum(parts[:, :, :share], axis=0)


def shards(coulomb_blocks, occupancy, green_occ, green_virt):
    naux, mu_rows, nao = coulomb_blocks.shape
    ranks = lax.axis_size("orb")
    planes = lax.axis_size("aux")
    share = naux // planes
    own = screen(coulomb_blocks, occupancy, share)
    own_virt, got = fetch_virt(green_virt)
    screened = lax.all_to_all(own, "orb", split_axis=0, concat_axis=0, tiled=True).reshape(nao, nao)
    half_occ = apply_occ(green_occ, screened)
    half_occ, *late = lax.optimization_barrier((half_occ, *got))
    half_rows = apply_virt(coulomb_blocks, occupancy, own_virt, [*late, *swap_cores(late)])
    returned = lax.all_to_all(half_occ.reshape(ranks, mu_rows, nao), "orb", split_axis=0, concat_axis=0, tiled=True)
    partial_pol = contract(half_rows, returned)
    parts = partial_pol.reshape(ranks, naux // ranks, LANES)
    parts = lax.all_to_all(parts, "orb", split_axis=0, concat_axis=0, tiled=True)
    return finish(parts, share).T


def solution(mesh):
    in_specs = (P(None, "orb", None), P("orb", None), P(), P(None, "aux"))
    out_specs = P("aux", "orb")
    return jax.shard_map(shards, mesh=mesh, in_specs=in_specs, out_specs=out_specs, check_vma=False)
```

```python
import functools

import jax
import jax.numpy as jnp
from jax import lax
from jax.experimental import pallas as pl
from jax.experimental.pallas import tpu as pltpu
from jax.sharding import PartitionSpec as P

BLK = 8
LANES = 128
SCREEN_FLOPS = 1000
ALL_VMEM = 60 * 1024 * 1024
MOST_VMEM = 48 * 1024 * 1024
WIDE_VMEM = 10 * 1024 * 1024
PART = 64
PRODUCT_VMEM = 56 * 1024 * 1024
VMEM = pl.BlockSpec(memory_space=pltpu.VMEM)
ANY = pl.BlockSpec(memory_space=pl.ANY)


def expand(occupancy, rows, cols):
    blocks = occupancy.shape[1]
    block = lax.broadcasted_iota(jnp.int32, (blocks, cols), 0)
    col = lax.broadcasted_iota(jnp.int32, (blocks, cols), 1)
    spread = (lax.div(col, BLK) == block).astype(jnp.float32)
    wide = jnp.dot(occupancy.astype(jnp.float32), spread, preferred_element_type=jnp.float32)
    return jnp.concatenate([jnp.broadcast_to(wide[i : i + 1], (BLK, cols)) for i in range(rows // BLK)], axis=0)


def screen_kernel(coulomb_ref, occupancy_ref, out_ref, part, occupancy, in_sem, out_sem, occupancy_sem):
    share, rows, cols = part.shape
    chunks = in_sem.shape[0]
    block = share // chunks
    first = lax.axis_index("aux") * share

    def fetch(i):
        return pltpu.make_async_copy(
            coulomb_ref.at[pl.ds(first + i * block, block)], part.at[pl.ds(i * block, block)], in_sem.at[i]
        )

    def put(i):
        here = pl.ds(i * block, block)
        return pltpu.make_async_copy(part.at[here], out_ref.at[here], out_sem.at[i])

    copy = pltpu.make_async_copy(occupancy_ref, occupancy, occupancy_sem)
    copy.start()
    for i in range(chunks):
        fetch(i).start()
    copy.wait()
    mask = expand(occupancy[...], rows, cols).astype(part.dtype)

    @pl.loop(0, chunks)
    def _(i):
        fetch(i).wait()
        here = pl.ds(i * block, block)
        part[here] = part[here] * mask[None]
        put(i).start()

    @pl.loop(0, chunks)
    def _(i):
        put(i).wait()


def screen(coulomb_blocks, occupancy, share, chunks=4):
    part = (share, *coulomb_blocks.shape[1:])
    dtype = coulomb_blocks.dtype
    return pl.pallas_call(
        screen_kernel,
        in_specs=[ANY, ANY],
        out_specs=ANY,
        out_shape=jax.ShapeDtypeStruct(part, dtype),
        scratch_shapes=[
            pltpu.VMEM(part, dtype),
            pltpu.VMEM(occupancy.shape, occupancy.dtype),
            pltpu.SemaphoreType.DMA((chunks,)),
            pltpu.SemaphoreType.DMA((chunks,)),
            pltpu.SemaphoreType.DMA,
        ],
        compiler_params=pltpu.CompilerParams(vmem_limit_bytes=ALL_VMEM),
        name="screen",
    )(coulomb_blocks, occupancy)


def fetch_virt(green_virt):
    ranks = lax.axis_size("aux")
    orbs = lax.axis_size("orb")
    own = green_virt.T
    half = own.shape[0] // 2
    own_half = lax.dynamic_slice_in_dim(own, lax.rem(lax.axis_index("orb"), 2) * half, half, 0)
    got = {}
    for dist in range(ranks // 2, 0, -1):
        pairs = []
        for orb in range(orbs):
            for aux in range(ranks):
                target = (aux - dist if orb % 2 == 0 else aux + dist) % ranks
                pairs.append((orb * ranks + aux, orb * ranks + target))
        got[dist] = lax.ppermute(own if 2 * dist < ranks else own_half, ("orb", "aux"), pairs)
    return own, [got[dist] for dist in sorted(got)]


def swap_cores(blocks):
    pairs = [(i, i ^ 1) for i in range(lax.axis_size("orb"))]
    return [lax.ppermute(block, "orb", pairs) for block in blocks]


def assemble(ranks, own_ref, block_refs, virt):
    me, side = lax.axis_index("aux"), lax.rem(lax.axis_index("orb"), 2)
    cols = own_ref.shape[0]
    far = ranks // 2
    virt[pl.ds(pl.multiple_of(me * cols, cols), cols), :] = own_ref[...]
    for which in range(2):
        core = side if which == 0 else 1 - side
        for dist in range(1, far + 1):
            ref = block_refs[which * far + dist - 1]
            source = lax.rem(me + ranks + jnp.where(core == 0, dist, -dist), ranks)
            first = source * cols + (core * (cols // 2) if 2 * dist == ranks else 0)
            virt[pl.ds(pl.multiple_of(first, cols // 2), ref.shape[0]), :] = ref[...]


def apply_virt_kernel(ranks, coulomb_ref, occupancy_ref, own_ref, *refs):
    (*block_refs, out_ref, virt, mask) = refs
    rows, count, cols = out_ref.shape

    @pl.when(pl.program_id(0) == 0)
    def _():
        once = expand(occupancy_ref[...], rows, cols)
        mask[...] = jnp.concatenate([once, once], axis=0).astype(mask.dtype)
        assemble(ranks, own_ref, block_refs, virt)

    @pl.loop(0, count // PART)
    def _(i):
        here = pl.ds(pl.multiple_of(i * PART * rows, PART * rows), PART * rows)
        screened = coulomb_ref[here, :].reshape(PART // 2, 2 * rows, cols) * mask[...][None]
        half = jnp.dot(screened.reshape(PART * rows, cols), virt[...], preferred_element_type=jnp.float32)
        half = half.reshape(PART, rows, cols).astype(out_ref.dtype)
        out_ref[:, pl.ds(pl.multiple_of(i * PART, PART), PART), :] = jnp.swapaxes(half, 0, 1)


def apply_virt(coulomb_blocks, occupancy, own, blocks, count=64):
    naux, rows, cols = coulomb_blocks.shape
    dtype = coulomb_blocks.dtype
    ranks = lax.axis_size("aux")
    return pl.pallas_call(
        functools.partial(apply_virt_kernel, ranks),
        grid=(naux // count,),
        in_specs=[
            pl.BlockSpec((count * rows, cols), lambda i: (i, 0)),
            pl.BlockSpec(occupancy.shape, lambda i: (0, 0)),
            *[VMEM] * (1 + len(blocks)),
        ],
        out_specs=pl.BlockSpec((rows, count, cols), lambda i: (0, i, 0)),
        out_shape=jax.ShapeDtypeStruct((2 * rows, naux, cols), dtype),
        scratch_shapes=[pltpu.VMEM((ranks * own.shape[0], cols), dtype), pltpu.VMEM((2 * rows, cols), dtype)],
        compiler_params=pltpu.CompilerParams(vmem_limit_bytes=PRODUCT_VMEM),
        name="apply_virt",
    )(coulomb_blocks.reshape(naux * rows, cols), occupancy, own, *blocks)


def apply_occ_kernel(occ_ref, screened_ref, out_ref, half, sem):
    chunks = sem.shape[0]
    block = half.shape[0] // chunks
    copies = []
    for i in range(chunks):
        here = pl.ds(i * block, block)
        half[here, :] = jnp.dot(
            occ_ref[here, :], screened_ref[...], preferred_element_type=jnp.float32
        ).astype(half.dtype)
        copies.append(pltpu.make_async_copy(half.at[here], out_ref.at[here], sem.at[i]))
        copies[-1].start()
    for copy in copies:
        copy.wait()


def apply_occ(green_occ, screened, chunks=3):
    return pl.pallas_call(
        apply_occ_kernel,
        in_specs=[VMEM] * 2,
        out_specs=ANY,
        out_shape=jax.ShapeDtypeStruct(screened.shape, screened.dtype),
        scratch_shapes=[pltpu.VMEM(screened.shape, screened.dtype), pltpu.SemaphoreType.DMA((chunks,))],
        compiler_params=pltpu.CompilerParams(vmem_limit_bytes=WIDE_VMEM),
        name="apply_occ",
    )(green_occ, screened)


def contract_kernel(returned_ref, half_ref, out_ref, left, right, sem):
    rows, naux, cols = left.shape
    share = right.shape[1]
    chunks = sem.shape[0]
    depth = rows // chunks

    def fetch(i):
        here = pl.ds(i * depth, depth)
        return pltpu.make_async_copy(half_ref.at[here], left.at[here], sem.at[i])

    for i in range(chunks):
        fetch(i).start()

    @pl.loop(0, share // 16)
    def _(i):
        here = pl.ds(pl.multiple_of(i * 16, 16), 16)
        right[:, here, :] = jnp.swapaxes(returned_ref[here], 0, 1)

    out_ref[...] = jnp.zeros(out_ref.shape, out_ref.dtype)

    @pl.loop(0, chunks)
    def _(i):
        fetch(i).wait()
        total = jnp.zeros((naux, share), jnp.float32)
        for j in range(depth):
            total += lax.dot_general(
                left[i * depth + j], right[i * depth + j], (((1,), (1,)), ((), ())), preferred_element_type=jnp.float32
            )
        out_ref[:, :share] += total


def contract(half_rows, returned, chunks=3):
    _, naux, cols = half_rows.shape
    share, rows, _ = returned.shape
    dtype = half_rows.dtype
    return pl.pallas_call(
        contract_kernel,
        in_specs=[VMEM, ANY],
        out_specs=VMEM,
        out_shape=jax.ShapeDtypeStruct((naux, LANES), jnp.float32),
        scratch_shapes=[
            pltpu.VMEM((rows, naux, cols), dtype),
            pltpu.VMEM((rows, share, cols), dtype),
            pltpu.SemaphoreType.DMA((chunks,)),
        ],
        compiler_params=pltpu.CompilerParams(vmem_limit_bytes=MOST_VMEM),
        name="contract",
    )(returned, half_rows)


def finish(parts, share):
    return jnp.sum(parts[:, :, :share], axis=0)


def shards(coulomb_blocks, occupancy, green_occ, green_virt):
    naux, mu_rows, nao = coulomb_blocks.shape
    ranks = lax.axis_size("orb")
    planes = lax.axis_size("aux")
    share = naux // planes
    own = screen(coulomb_blocks, occupancy, share)
    own_virt, got = fetch_virt(green_virt)
    screened = lax.all_to_all(own, "orb", split_axis=0, concat_axis=0, tiled=True).reshape(nao, nao)
    half_occ = apply_occ(green_occ, screened)
    half_occ, *late = lax.optimization_barrier((half_occ, *got))
    half_rows = apply_virt(coulomb_blocks, occupancy, own_virt, [*late, *swap_cores(late)])
    returned = lax.all_to_all(half_occ.reshape(ranks, mu_rows, nao), "orb", split_axis=0, concat_axis=0, tiled=True)
    partial_pol = contract(half_rows, returned)
    parts = partial_pol.reshape(ranks, naux // ranks, LANES)
    parts = lax.all_to_all(parts, "orb", split_axis=0, concat_axis=0, tiled=True)
    return finish(parts, share).T


def solution(mesh):
    in_specs = (P(None, "orb", None), P("orb", None), P(), P(None, "aux"))
    out_specs = P("aux", "orb")
    return jax.shard_map(shards, mesh=mesh, in_specs=in_specs, out_specs=out_specs, check_vma=False)
```
